32 devices in a mesh: row: 4 (over x, core), col: 8 (over z, y).
Axes of the slice: x: 2, y: 2, z: 4, core: 2. Of those that a mesh axis runs over, the one named last changes fastest.
Arguments:
- act_values: bfloat16 [512, 16384], P('col', 'row'), may hold values from -6 to 6
- act_scales: float32 [512, 128], P('col', 'row'), may hold values from 0.3 to 4
- grad_values: bfloat16 [512, 28672], P('row', 'col'), may hold values from -6 to 6
- grad_scales: float32 [512, 224], P('row', 'col'), may hold values from 0.3 to 4
- weight: bfloat16 [16384, 28672], P('row', 'col'), may hold values from -0.03125 to 0.03125
Outputs:
- input_grad: bfloat16 [512, 16384], P('col', 'row')
- weight_grad: bfloat16 [16384, 28672], P('row', 'col')
The draws below stay inside these ranges and needn't reach their ends.
All inputs are finite; a program needn't handle non-finite values.
Results may differ from the reference program's by a relative error of at most 0.015.
Values may be sent and summed in bfloat16 or wider, within the bound.
A program may use at most 128 MiB of HBM per device.

```python
import math
import jax
import jax.numpy as jnp
from jax import lax

D = 16384
FF = 28672
QB = 128
TOKENS = 512
N_COL = 8


def with_spikes(drawn, rng, source, target, parts, factor):
    owner, partner = [(jnp.arange(drawn.shape[dim]) // (drawn.shape[dim] // parts)).reshape([-1 if axis == dim else 1 for axis in range(drawn.ndim)]) for dim in (source, target)]
    chosen = jax.random.permutation(rng, parts)[partner]
    strong = (owner == chosen) | (owner == (partner + parts // 2) % parts)
    return jnp.where(strong, factor * drawn, drawn)


def block_levels(rng, dims, shards, least, top_value):
    loudness = 1.0
    for position, parts in shards:
        heights = jax.random.uniform(jax.random.fold_in(jax.random.fold_in(rng, 6), position), (parts,), jnp.float32, least / len(shards), top_value / len(shards))
        loudness = loudness * jnp.repeat(jnp.exp(heights), dims[position] // parts).reshape((-1,) + (1,) * (len(dims) - 1 - position))
    return loudness


def scatter_about(key, dims, scale, reach, cuts=(), kind=jnp.bfloat16):
    array = jax.random.normal(key, dims, jnp.float32) * scale
    if len(cuts) > 0:
        array = block_levels(key, dims, cuts, -0.22, 0.18) * array
    return jnp.clip(array, min=-reach, max=reach).astype(kind)


def gaussian_with(own_key, extent, width, most, cuts, heavy, kind=jnp.bfloat16):
    values = width * jax.random.normal(own_key, extent, jnp.float32)
    if cuts:
        values = values * block_levels(own_key, extent, cuts, -0.22, 0.18)
    return jnp.clip(with_spikes(values, jax.random.fold_in(own_key, 3), *heavy), -most, most).astype(kind)


def setup_inputs(seed: int = 0) -> dict:
    keys = jax.random.split(jax.random.key(seed), 6)
    return {
        "act_values": scatter_about(keys[0], (TOKENS, D), 1.0, 6.0, ((0, 8), (1, 4))),
        "act_scales": jnp.clip(jnp.exp(math.log(4.0) - 2.5902671 * jax.random.uniform(keys[1], (TOKENS, D // QB), jnp.float32) ** block_levels(keys[1], (TOKENS, D // QB), ((0, 8), (1, 4)), -0.2, 0.2)), 0.3, 4.0),
        "grad_values": gaussian_with(keys[2], (TOKENS, FF), 1.0, 6.0, ((0, 4), (1, 8)), (1, 0, 8, 2.0)),
        "grad_scales": jnp.clip(jnp.exp(math.log(4.0) - 2.5902671 * jax.random.uniform(keys[3], (TOKENS, FF // QB), jnp.float32) ** block_levels(keys[3], (TOKENS, FF // QB), ((0, 4), (1, 8)), -0.2, 0.2)), 0.3, 4.0),
        "weight": scatter_about(keys[4], (D, FF), FF ** -0.5, 0.03125, ((0, 4), (1, 8))),
    }


def dequantize(values, scales):
    height, breadth = values.shape
    scaled = values.astype(jnp.float32).reshape(height, breadth // QB, QB) * scales[:, :, None]
    return scaled.reshape(height, breadth).astype(jnp.bfloat16)


def reference(act_values, act_scales, grad_values, grad_scales, weight):
    activations = dequantize(act_values, act_scales)
    gradients = dequantize(grad_values, grad_scales)
    weight_grad = lax.dot_general(activations, gradients, (((0,), (0,)), ((), ())), preferred_element_type=jnp.float32).astype(jnp.bfloat16)
    slab_width = FF // N_COL

    def accumulate(running, column):
        offset = column * slab_width
        grad_slab = lax.dynamic_slice_in_dim(gradients, offset, slab_width, 1)
        weight_slab = lax.dynamic_slice_in_dim(weight, offset, slab_width, 1)
        partial_block = lax.dot_general(grad_slab, weight_slab, (((1,), (1,)), ((), ())), preferred_element_type=jnp.float32).astype(jnp.bfloat16)
        partial_block = lax.optimization_barrier(partial_block)
        return running + partial_block.astype(jnp.float32), None

    summed, _ = lax.scan(accumulate, jnp.zeros((TOKENS, D), jnp.float32), jnp.arange(N_COL, dtype=jnp.int32))
    return summed.astype(jnp.bfloat16), weight_grad
```

```python
import functools

import jax
import jax.numpy as jnp
from jax import lax
from jax.experimental import pallas as pl
from jax.experimental.pallas import tpu as pltpu
from jax.sharding import PartitionSpec as P

QB = 128
PIECES = 4
SUBS = 2
LATE = 3
MESH = pl.DeviceIdType.MESH


def kernel(n_row, n_col, act_v, act_s, grad_v, grad_s, weight, out, act_all, grad_all,
           own, grads, wv, part, got, ag_send, ag_recv, rs_send, rs_recv,
           g_send, g_recv, w_sem, local_sem):
    row, col = lax.axis_index("row"), lax.axis_index("col")
    n_x, n_z = n_row // 2, n_col // 2
    core, x = row % 2, row // 2
    tb, width = act_v.shape
    half = width // 2
    sub = half // SUBS
    piece = half // PIECES
    tr = grad_v.shape[0]

    def to_col(q):
        q = lax.rem(q + 2 * n_col, n_col)
        back = q // n_z
        return (1 - back) * 2 * q + back * (2 * (n_col - 1 - q) + 1)

    z, y = col // 2, col % 2
    pos = z + y * (n_col - 1 - 2 * z)
    nexts = (to_col(pos + 1), to_col(pos - 1))
    sign = (1, -1)
    mate = x * 2 + (1 - core)

    def tokens(q):
        return pl.ds(pl.multiple_of(to_col(q) * tb, tb), tb)

    def ag(s, d, u, incoming=False, first=False):
        q = pos - sign[d] * s - (sign[d] if incoming else 0)
        cols = pl.ds(d * half + u * sub, sub)
        dst = act_all.at[tokens(q), cols]
        return pltpu.make_async_remote_copy(
            src_ref=own.at[:, cols] if first else dst,
            dst_ref=dst,
            send_sem=ag_send.at[s, d, u],
            recv_sem=ag_recv.at[s, d, u],
            device_id={"row": row, "col": nexts[d]},
            device_id_type=MESH,
        )

    def ag_forward(s):
        for u in range(SUBS):
            for d in range(2):
                ag(s - 1, d, u, incoming=True).wait_recv()
                ag(s, d, u).start()

    def rs(s, i, first=False):
        d = i // PIECES
        q = pos - sign[d] * (1 + s)
        return pltpu.make_async_remote_copy(
            src_ref=part.at[i, tokens(q)] if first else got.at[s - 1, i],
            dst_ref=got.at[s, i],
            send_sem=rs_send.at[s, i],
            recv_sem=rs_recv.at[s, i],
            device_id={"row": row, "col": nexts[d]},
            device_id_type=MESH,
        )

    def shard(r):
        return pl.ds(pl.multiple_of(r * tr, tr), tr)

    def g(k):
        if k == 0:
            src, to = row, mate
        elif k < n_x:
            src, to = row, ((x + k) % n_x) * 2 + core
        else:
            src, to = ((x - (k - n_x + 1) + n_x) % n_x) * 2 + core, mate
        ref = grads.at[shard(src)]
        return pltpu.make_async_remote_copy(
            src_ref=ref, dst_ref=ref, send_sem=g_send.at[k], recv_sem=g_recv.at[k],
            device_id={"row": to, "col": col}, device_id_type=MESH,
        )

    def load(i):
        return pltpu.make_async_copy(
            weight.at[pl.ds(pl.multiple_of(i * piece, piece), piece)], wv.at[i], w_sem.at[i]
        )

    barrier = pltpu.get_barrier_semaphore()
    peers = [{"row": row, "col": nexts[0]}, {"row": row, "col": nexts[1]}, {"row": mate, "col": col}]
    peers += [{"row": ((x + k) % n_x) * 2 + core, "col": col} for k in range(1, n_x)]
    for peer in peers:
        pl.semaphore_signal(barrier, inc=1, device_id=peer, device_id_type=MESH)

    for j in range(width // QB):
        at = slice(j * QB, (j + 1) * QB)
        own[:, at] = (act_v[:, at].astype(jnp.float32) * act_s[:, j:j + 1]).astype(own.dtype)
    for j in range(grad_v.shape[1] // QB):
        at = slice(j * QB, (j + 1) * QB)
        grads[shard(row), at] = (
            grad_v[:, at].astype(jnp.float32) * grad_s[:, j:j + 1]
        ).astype(grads.dtype)

    pl.semaphore_wait(barrier, len(peers))
    for k in range(1, n_x):
        g(k).start()
    for u in range(SUBS):
        for d in range(2):
            ag(0, d, u, first=True).start()
    g(0).start()
    keep = pltpu.make_async_copy(own, act_all.at[tokens(pos)], local_sem.at[0])
    keep.start()
    for i in range(2 * PIECES):
        load((i % 2) * PIECES + i // 2).start()

    def early(s, carry):
        ag_forward(s)
        return carry

    lax.fori_loop(1, n_col - 1 - LATE, early, 0)

    for k in range(1, n_x):
        g(k).wait_recv()
        g(n_x - 1 + k).start()
    g(0).wait_recv()
    for k in range(1, n_x):
        g(n_x - 1 + k).wait_recv()
    store = pltpu.make_async_copy(grads, grad_all, local_sem.at[1])
    store.start()

    def product(k, carry):
        for d in range(2):
            i = d * PIECES + k
            load(i).wait()
            part[i] = lax.dot_general(
                grads[...], wv[i], (((1,), (1,)), ((), ())), preferred_element_type=jnp.float32
            ).astype(part.dtype)
            rs_first(i, d).start()

        @pl.when(k < LATE)
        def _():
            ag_forward(n_col - 1 - LATE + k)

        return carry

    def rs_first(i, d):
        return pltpu.make_async_remote_copy(
            src_ref=part.at[i, tokens(pos - sign[d])],
            dst_ref=got.at[0, i],
            send_sem=rs_send.at[0, i],
            recv_sem=rs_recv.at[0, i],
            device_id={"row": row, "col": nexts[d]},
            device_id_type=MESH,
        )

    lax.fori_loop(0, PIECES, product, 0)

    order = [d * PIECES + k for k in range(PIECES) for d in range(2)]

    def total(s, i):
        q = pos - sign[i // PIECES] * (2 + s)
        return (got[s, i].astype(jnp.float32) + part[i, tokens(q)].astype(jnp.float32)).astype(out.dtype)

    def reduce(s, carry):
        for i in order:
            wait_got(s, i)
            got[s, i] = total(s, i)
            rs(s + 1, i).start()
        return carry

    def wait_got(s, i):
        pltpu.make_async_remote_copy(
            src_ref=got.at[s, i], dst_ref=got.at[s, i],
            send_sem=rs_send.at[s, i], recv_sem=rs_recv.at[s, i],
            device_id={"row": row, "col": nexts[i // PIECES]}, device_id_type=MESH,
        ).wait_recv()

    lax.fori_loop(0, n_col - 2, reduce, 0)
    for i in order:
        wait_got(n_col - 2, i)
        out[:, i * piece:(i + 1) * piece] = total(n_col - 2, i)

    for u in range(SUBS):
        for d in range(2):
            ag(n_col - 2, d, u, incoming=True).wait_recv()
            ag(0, d, u, first=True).wait_send()
    for i in order:
        rs(0, i, first=True).wait_send()

    def drain(s, carry):
        for u in range(SUBS):
            for d in range(2):
                ag(s, d, u).wait_send()
        for i in order:
            rs(s, i).wait_send()
        return carry

    lax.fori_loop(1, n_col - 1, drain, 0)
    for k in range(2 * n_x - 1):
        g(k).wait_send()
    keep.wait()
    store.wait()


def shards(mesh, act_values, act_scales, grad_values, grad_scales, weight):
    n_row, n_col = mesh.shape["row"], mesh.shape["col"]
    tb, width = act_values.shape
    tr, hidden = grad_values.shape
    count = n_row * tr
    piece = width // 2 // PIECES
    dtype = act_values.dtype
    vmem = pl.BlockSpec(memory_space=pltpu.VMEM)
    anywhere = pl.BlockSpec(memory_space=pl.ANY)
    dma = pltpu.SemaphoreType.DMA
    summed, activations, gradients = pl.pallas_call(
        functools.partial(kernel, n_row, n_col),
        out_shape=(
            jax.ShapeDtypeStruct((tb, width), dtype),
            jax.ShapeDtypeStruct((count, width), dtype),
            jax.ShapeDtypeStruct((count, hidden), dtype),
        ),
        in_specs=[vmem, vmem, vmem, vmem, anywhere],
        out_specs=(vmem, anywhere, anywhere),
        scratch_shapes=[
            pltpu.VMEM((tb, width), dtype),
            pltpu.VMEM((count, hidden), dtype),
            pltpu.VMEM((2 * PIECES, piece, hidden), dtype),
            pltpu.VMEM((2 * PIECES, count, piece), dtype),
            pltpu.VMEM((n_col - 1, 2 * PIECES, tb, piece), dtype),
            dma((n_col - 1, 2, SUBS)),
            dma((n_col - 1, 2, SUBS)),
            dma((n_col - 1, 2 * PIECES)),
            dma((n_col - 1, 2 * PIECES)),
            dma((n_row - 1,)),
            dma((n_row - 1,)),
            dma((2 * PIECES,)),
            dma((2,)),
        ],
        compiler_params=pltpu.CompilerParams(
            collective_id=0, has_side_effects=True, vmem_limit_bytes=58 * 1024 * 1024
        ),
        cost_estimate=pl.CostEstimate(
            flops=2 * count * width * hidden,
            bytes_accessed=2 * width * hidden,
            transcendentals=0,
        ),
    )(act_values, act_scales, grad_values, grad_scales, weight)
    weight_grad = lax.dot_general(
        activations, gradients, (((0,), (0,)), ((), ())), preferred_element_type=jnp.float32
    ).astype(jnp.bfloat16)
    return (summed, weight_grad)


def solution(mesh):
    placed = (P("col", "row"), P("col", "row"), P("row", "col"), P("row", "col"), P("row", "col"))
    return jax.shard_map(
        functools.partial(shards, mesh),
        mesh=mesh,
        in_specs=placed,
        out_specs=(P("col", "row"), P("row", "col")),
        check_vma=False,
    )
```
